32 devices in a mesh: sample: 2 (over x), ctx: 16 (over z, y, core).
Axes of the slice: x: 2, y: 2, z: 4, core: 2. Of those that a mesh axis runs over, the one named last changes fastest.
Arguments:
- queries: bfloat16 [4, 512, 8192], P('sample', None, 'ctx'), may hold values from -8 to 8
- prompt_key_value: bfloat16 [2, 512, 1024], P(None, 'ctx', 'sample'), may hold values from -6 to 6
- continuation_key_value: bfloat16 [2, 4, 512, 1024], P(None, 'sample', 'ctx'), may hold values from -6 to 6
- page_owner: int32 [512], replicated, may hold values from 0 to 4, as said below
- cont_lengths: int32 [4], replicated, may hold values from 2 to 512, as said below
- branch_offsets: int32 [4], replicated, may hold values from 128 to 512
Outputs:
- attended: bfloat16 [4, 512, 8192], P('sample', None, 'ctx')
The draws below stay inside these ranges and needn't reach their ends.
Inputs may be any that keep to these rules, and one draw needn't show every extreme that they name: `page_owner`: constant over each aligned page of 16 positions; 0 marks a page seen by every continuation that branches after it, s + 1 a page seen only by continuation s; some page belongs to continuation 4 - 1. `cont_lengths`: some continuation has all 512 positions live.
All inputs are finite; a program needn't handle non-finite values.
Results may differ from the reference program's by a relative error of at most 0.0045.
Values may be sent and summed in bfloat16 or wider, within the bound.
A program may use at most 64 MiB of HBM per device.

```python
import jax
import jax.numpy as jnp
from jax import lax

QUERY_HEADS = 64
KEY_VALUE_HEADS = 8
HEAD_SIZE = 128
CONTINUATION_LEN = 512
PAGE = 16
SAMPLE_COUNT = 4
PROMPT_LEN = 512


def draw_queries(key, part):
    gaussian_portion = jax.random.normal(jax.random.fold_in(key, 11), (SAMPLE_COUNT, CONTINUATION_LEN, QUERY_HEADS * HEAD_SIZE), jnp.float32)
    result = jnp.clip(2.0 * gaussian_portion, -8.0, 8.0)
    return result.astype(jnp.bfloat16)


def draw_continuation_key_value(key, part):
    gaussian_portion = jax.random.normal(jax.random.fold_in(key, 22), (2, SAMPLE_COUNT, CONTINUATION_LEN, KEY_VALUE_HEADS * HEAD_SIZE), jnp.float32)
    result = jnp.clip(gaussian_portion, -6.0, 6.0)
    return result.astype(jnp.bfloat16)


def draw_page_owner(key, part):
    page_count = PROMPT_LEN // PAGE
    shared = jax.random.randint(jax.random.fold_in(key, 44), (page_count,), 0, 2)
    private = jax.random.randint(jax.random.fold_in(key, 45), (page_count,), 1, SAMPLE_COUNT + 1)
    per_page = jnp.where(shared == 0, 0, private)
    chosen = jax.random.randint(jax.random.fold_in(key, 46), (), 0, page_count)
    per_page = jnp.where(jnp.arange(page_count) == chosen, SAMPLE_COUNT, per_page)
    return jnp.repeat(per_page, PAGE).astype(jnp.int32)


def draw_cont_lengths(key, part):
    picked_len = jax.random.randint(jax.random.fold_in(key, 33), (SAMPLE_COUNT,), 2, CONTINUATION_LEN + 1)
    chosen = jax.random.randint(jax.random.fold_in(key, 34), (), 0, SAMPLE_COUNT)
    return jnp.where(jnp.arange(SAMPLE_COUNT) == chosen, CONTINUATION_LEN, picked_len).astype(jnp.int32)


def plant(drawn, stream_key, low, largest):
    index_at = [jax.random.randint(jax.random.fold_in(stream_key, axis), (), 0, length) for axis, length in enumerate(drawn.shape)]
    widest = drawn.shape.index(max(drawn.shape))
    beside = index_at[:widest] + [(index_at[widest] + 1) % drawn.shape[widest]] + index_at[widest + 1:]
    return drawn.at[tuple(index_at)].set(low).at[tuple(beside)].set(largest)


def steps_of(stream_key, extent, pieces, smallest, high):
    def one(position, parts):
        steps = jax.random.uniform(jax.random.fold_in(jax.random.fold_in(stream_key, 6), position), (parts,), jnp.float32, smallest / len(pieces), high / len(pieces))
        return jnp.repeat(jnp.exp(steps), extent[position] // parts).reshape((-1,) + (1,) * (len(extent) - position - 1))

    gain = one(*pieces[0])
    for cut in pieces[1:]:
        gain = gain * one(*cut)
    return gain


def normal_values(key, dims, width, reach, cuts=(), held_as=jnp.bfloat16):
    drawn = width * jax.random.normal(key, dims, jnp.float32)
    if cuts:
        drawn = drawn * steps_of(key, dims, cuts, -0.22, 0.18)
    return jnp.clip(drawn, -reach, reach).astype(held_as)


def setup_inputs(seed: int = 0) -> dict:
    streams_of = jax.random.split(jax.random.key(seed), 7)
    return {
        "queries": draw_queries(jax.random.fold_in(streams_of[6], 71), 0),
        "prompt_key_value": normal_values(streams_of[1], (2, PROMPT_LEN, KEY_VALUE_HEADS * HEAD_SIZE), 1.0, 6.0, ((1, 16), (2, 2))),
        "continuation_key_value": draw_continuation_key_value(jax.random.fold_in(streams_of[6], 71), 0),
        "page_owner": draw_page_owner(jax.random.fold_in(streams_of[6], 71), 0),
        "cont_lengths": draw_cont_lengths(jax.random.fold_in(streams_of[6], 71), 0),
        "branch_offsets": plant(jax.random.randint(streams_of[5], (SAMPLE_COUNT,), PROMPT_LEN // 4, PROMPT_LEN + 1), jax.random.fold_in(streams_of[5], 1), PROMPT_LEN // 4, PROMPT_LEN).astype(jnp.int32),
    }


def reference(queries, prompt_key_value, continuation_key_value, page_owner, cont_lengths, branch_offsets):
    query_groups = QUERY_HEADS // KEY_VALUE_HEADS
    scale = HEAD_SIZE ** -0.5
    query_matrix = queries.reshape(SAMPLE_COUNT, CONTINUATION_LEN, KEY_VALUE_HEADS, query_groups, HEAD_SIZE).transpose(0, 2, 1, 3, 4).reshape(SAMPLE_COUNT * KEY_VALUE_HEADS, CONTINUATION_LEN * query_groups, HEAD_SIZE)
    prompt_key_rows = prompt_key_value[0].reshape(PROMPT_LEN, KEY_VALUE_HEADS, HEAD_SIZE).transpose(1, 0, 2)
    prompt_value_rows = prompt_key_value[1].reshape(PROMPT_LEN, KEY_VALUE_HEADS, HEAD_SIZE).transpose(1, 0, 2)
    continuation_keys = continuation_key_value[0].reshape(SAMPLE_COUNT, CONTINUATION_LEN, KEY_VALUE_HEADS, HEAD_SIZE).transpose(0, 2, 1, 3)
    continuation_values = continuation_key_value[1].reshape(SAMPLE_COUNT, CONTINUATION_LEN, KEY_VALUE_HEADS, HEAD_SIZE).transpose(0, 2, 1, 3)
    prompt_pos = jnp.arange(PROMPT_LEN, dtype=jnp.int32)
    cont_pos = jnp.arange(CONTINUATION_LEN, dtype=jnp.int32)
    row_pos = jnp.arange(CONTINUATION_LEN * query_groups, dtype=jnp.int32) // query_groups

    def single_head(flattened_index):
        sample_number = flattened_index // KEY_VALUE_HEADS
        head_number = flattened_index % KEY_VALUE_HEADS
        rows = query_matrix[flattened_index]
        keys_all = jnp.concatenate([prompt_key_rows[head_number], continuation_keys[sample_number, head_number]], axis=0)
        values_all = jnp.concatenate([prompt_value_rows[head_number], continuation_values[sample_number, head_number]], axis=0)
        scores = jnp.dot(rows, keys_all.T, preferred_element_type=jnp.float32) * scale
        owner_ok = (page_owner == 0) | (page_owner == sample_number + 1)
        prompt_seen = (prompt_pos < branch_offsets[sample_number]) & owner_ok
        length = cont_lengths[sample_number]
        cont_seen = (cont_pos[None, :] <= row_pos[:, None]) & (cont_pos[None, :] < length)
        visible = jnp.concatenate([jnp.broadcast_to(prompt_seen[None, :], (CONTINUATION_LEN * query_groups, PROMPT_LEN)), cont_seen], axis=1)
        masked = jnp.where(visible, scores, -1.0e30)
        row_max = jnp.max(masked, axis=1, keepdims=True)
        weights = jnp.where(visible, jnp.exp(masked - row_max), 0.0)
        weight_sum = jnp.sum(weights, axis=1, keepdims=True)
        mixed = jnp.dot(weights.astype(jnp.bfloat16), values_all, preferred_element_type=jnp.float32) / weight_sum
        return jnp.where((row_pos < length)[:, None], mixed, 0.0)

    output_rows = lax.map(single_head, jnp.arange(SAMPLE_COUNT * KEY_VALUE_HEADS, dtype=jnp.int32))
    output_rows = output_rows.reshape(SAMPLE_COUNT, KEY_VALUE_HEADS, CONTINUATION_LEN, query_groups, HEAD_SIZE).transpose(0, 2, 1, 3, 4)
    return output_rows.reshape(SAMPLE_COUNT, CONTINUATION_LEN, QUERY_HEADS * HEAD_SIZE).astype(jnp.bfloat16)
```

```python
import functools
import math

import jax
import jax.numpy as jnp
from jax import lax
from jax.experimental import pallas as pl
from jax.experimental.pallas import tpu as pltpu
from jax.sharding import PartitionSpec as P

KEY_VALUE_HEADS = 8
HEAD_SIZE = 128
MESH = pl.DeviceIdType.MESH

neg_large = -1e30
query_block = 128


def gather_kernel(
    samples,
    ctx,
    prompt_ref,
    cont_ref,
    own_prompt,
    own_cont,
    prompt_send,
    prompt_forward,
    prompt_recv,
    cont_send,
    cont_forward,
    cont_recv,
):
    groups = KEY_VALUE_HEADS
    copies = ctx // groups
    shard_heads = prompt_ref.shape[2] // HEAD_SIZE
    sample = lax.axis_index("sample")
    me = lax.axis_index("ctx")
    group = me // copies
    rank = lax.rem(me, copies)

    siblings = [group * copies + lax.rem(rank + k, copies) for k in range(1, copies)]

    barrier = pltpu.get_barrier_semaphore()
    count = 0
    for ds in range(samples):
        for j in range(groups):
            if ds == 0 and j == 0:
                continue
            peer = lax.rem(group + j, groups) * copies + rank
            pl.semaphore_signal(
                barrier,
                inc=1,
                device_id=(lax.rem(sample + ds, samples), peer),
                device_id_type=MESH,
            )
            count += 1
    for sibling in siblings:
        pl.semaphore_signal(
            barrier, inc=1, device_id=(sample, sibling), device_id_type=MESH
        )
        count += 1
    pl.semaphore_wait(barrier, count)

    def head_columns(head):
        return pl.ds(pl.multiple_of(head * HEAD_SIZE, HEAD_SIZE), HEAD_SIZE)

    sends = []

    def send(src, dst, send_sem, recv_sem, device_id):
        copy = pltpu.make_async_remote_copy(
            src_ref=src,
            dst_ref=dst,
            send_sem=send_sem,
            recv_sem=recv_sem,
            device_id=device_id,
            device_id_type=MESH,
        )
        copy.start()
        return copy

    own_piece = cont_ref.at[:, :, :, head_columns(group)]
    pltpu.make_async_copy(own_piece, own_cont.at[:, :, me], cont_recv.at[me]).start()

    for j in range(1, groups):
        target = lax.rem(group + j, groups)
        sends.append(
            send(
                cont_ref.at[:, :, :, head_columns(target)],
                own_cont.at[:, :, me],
                cont_send.at[j],
                cont_recv.at[me],
                (sample, target * copies + rank),
            )
        )
    own_shard = group // shard_heads
    for part in range(shard_heads):
        for ds in range(samples):
            local = lax.rem(part + group, shard_heads)
            head = sample * shard_heads + local
            target_sample = lax.rem(sample + ds, samples)
            src = prompt_ref.at[:, :, head_columns(local)]
            dst = own_prompt.at[:, me]
            index = part * samples + ds
            copy = pltpu.make_async_remote_copy(
                src_ref=src,
                dst_ref=dst,
                send_sem=prompt_send.at[index],
                recv_sem=prompt_recv.at[me],
                device_id=(target_sample, head * copies + rank),
                device_id_type=MESH,
            )
            if ds == 0:
                mine = head == group

                @pl.when(mine)
                def _():
                    pltpu.make_async_copy(src, dst, prompt_recv.at[me]).start()

                @pl.when(jnp.logical_not(mine))
                def _():
                    copy.start()

                sends.append((copy, jnp.logical_not(mine)))
            else:
                copy.start()
                sends.append(copy)

    for k, sibling in enumerate(siblings):
        sends.append(
            send(
                own_piece,
                own_cont.at[:, :, me],
                cont_forward.at[0, k],
                cont_recv.at[me],
                (sample, sibling),
            )
        )

    def wait_slot(buffer, sem):
        pltpu.make_async_copy(buffer, buffer, sem).wait()

    for j in range(groups):
        slot = lax.rem(group - j + groups, groups) * copies + rank
        wait_slot(own_prompt.at[:, slot], prompt_recv.at[slot])
        for k, sibling in enumerate(siblings):
            sends.append(
                send(
                    own_prompt.at[:, slot],
                    own_prompt.at[:, slot],
                    prompt_forward.at[j, k],
                    prompt_recv.at[slot],
                    (sample, sibling),
                )
            )
        wait_slot(own_cont.at[:, :, slot], cont_recv.at[slot])
        if j > 0:
            for k, sibling in enumerate(siblings):
                sends.append(
                    send(
                        own_cont.at[:, :, slot],
                        own_cont.at[:, :, slot],
                        cont_forward.at[j, k],
                        cont_recv.at[slot],
                        (sample, sibling),
                    )
                )

    for j in range(groups):
        for k in range(1, copies):
            other = lax.rem(rank + copies - k, copies)
            slot = lax.rem(group - j + groups, groups) * copies + other
            wait_slot(own_prompt.at[:, slot], prompt_recv.at[slot])
            wait_slot(own_cont.at[:, :, slot], cont_recv.at[slot])

    for item in sends:
        if isinstance(item, tuple):
            copy, started = item

            @pl.when(started)
            def _():
                copy.wait_send()
        else:
            item.wait_send()


def gather(prompt, cont, samples, ctx):
    groups = KEY_VALUE_HEADS
    copies = ctx // groups
    prompt_rows = prompt.shape[1]
    here, cont_rows = cont.shape[1:3]
    shard_heads = prompt.shape[2] // HEAD_SIZE
    forwards = max(copies - 1, 1)
    anywhere = pl.BlockSpec(memory_space=pl.ANY)
    own_prompt, own_cont = pl.pallas_call(
        functools.partial(gather_kernel, samples, ctx),
        out_shape=(
            jax.ShapeDtypeStruct((2, ctx, prompt_rows, HEAD_SIZE), prompt.dtype),
            jax.ShapeDtypeStruct((2, here, ctx, cont_rows, HEAD_SIZE), cont.dtype),
        ),
        in_specs=[anywhere, anywhere],
        out_specs=(anywhere, anywhere),
        scratch_shapes=[
            pltpu.SemaphoreType.DMA((shard_heads * samples,)),
            pltpu.SemaphoreType.DMA((groups, forwards)),
            pltpu.SemaphoreType.DMA((ctx,)),
            pltpu.SemaphoreType.DMA((groups,)),
            pltpu.SemaphoreType.DMA((groups, forwards)),
            pltpu.SemaphoreType.DMA((ctx,)),
        ],
        compiler_params=pltpu.CompilerParams(collective_id=0, has_side_effects=True),
        name="gather_heads",
    )(prompt, cont)
    own_prompt = own_prompt.reshape(2, ctx * prompt_rows, HEAD_SIZE)
    own_cont = own_cont.reshape(2, here, ctx * cont_rows, HEAD_SIZE)
    return own_prompt, own_cont


def attend_kernel(block, lengths, offsets, base, owner_ref, q_ref, prompt_ref, cont_ref, out_ref):
    heads = q_ref.shape[2] // HEAD_SIZE
    prompt_len = prompt_ref.shape[1]
    blocks = cont_ref.shape[2] // block
    sample = base[0] + pl.program_id(0)
    step = pl.program_id(1)
    length = lengths[sample]
    factor = HEAD_SIZE ** -0.5 * math.log2(math.e)
    contract_last = (((1,), (1,)), ((), ()))

    live = step * block < length

    @pl.when(jnp.logical_not(live))
    def _():
        out_ref[...] = jnp.zeros_like(out_ref)

    def with_ones(values):
        return jnp.concatenate([values, jnp.ones_like(values)], axis=1)

    for i in range(blocks):

        @pl.when(live & (step == i))
        def _():
            extent = (i + 1) * block
            q = jnp.concatenate(
                [q_ref[0, :, h * HEAD_SIZE : (h + 1) * HEAD_SIZE] for h in range(heads)], axis=0
            )
            owner = owner_ref[...]
            position = lax.broadcasted_iota(jnp.int32, (1, prompt_len), 1)
            seen = ((owner == 0) | (owner == sample + 1)) & (position < offsets[sample])
            bias = jnp.where(seen, 0.0, neg_large)
            first = lax.dot_general(
                q, prompt_ref[0], contract_last, preferred_element_type=jnp.float32
            )
            first = first + bias
            second = lax.dot_general(
                q, cont_ref[0, 0, :extent], contract_last, preferred_element_type=jnp.float32
            )
            row = lax.broadcasted_iota(jnp.int32, (block, block), 0)
            col = lax.broadcasted_iota(jnp.int32, (block, block), 1)
            causal = jnp.where(col <= row, 0.0, neg_large)
            causal = jnp.concatenate([causal] * heads, axis=0)
            diagonal = second[:, i * block :] + causal
            if i:
                second = jnp.concatenate([second[:, : i * block], diagonal], axis=1)
            else:
                second = diagonal
            row_max = jnp.maximum(
                jnp.max(first, axis=1, keepdims=True), jnp.max(second, axis=1, keepdims=True)
            )
            first = jnp.exp2((first - row_max) * factor).astype(jnp.bfloat16)
            second = jnp.exp2((second - row_max) * factor).astype(jnp.bfloat16)
            total = jnp.dot(
                first, with_ones(prompt_ref[1]), preferred_element_type=jnp.float32
            ) + jnp.dot(
                second, with_ones(cont_ref[1, 0, :extent]), preferred_element_type=jnp.float32
            )
            mixed = total[:, :HEAD_SIZE] / total[:, HEAD_SIZE:]
            place = i * block + lax.broadcasted_iota(jnp.int32, (block, HEAD_SIZE), 0)
            for h in range(heads):
                out_ref[0, :, h * HEAD_SIZE : (h + 1) * HEAD_SIZE] = jnp.where(
                    place < length, mixed[h * block : (h + 1) * block], 0.0
                ).astype(out_ref.dtype)


def attend(queries, own_prompt, own_cont, page_owner, lengths, offsets, base):
    here, cont_len, width = queries.shape
    prompt_len = own_prompt.shape[1]
    block = math.gcd(query_block, cont_len)
    return pl.pallas_call(
        functools.partial(attend_kernel, block),
        out_shape=jax.ShapeDtypeStruct(queries.shape, queries.dtype),
        grid_spec=pltpu.PrefetchScalarGridSpec(
            num_scalar_prefetch=3,
            grid=(here, cont_len // block),
            in_specs=[
                pl.BlockSpec((1, prompt_len), lambda s, i, *_: (0, 0)),
                pl.BlockSpec((1, block, width), lambda s, i, *_: (s, i, 0)),
                pl.BlockSpec((2, prompt_len, HEAD_SIZE), lambda s, i, *_: (0, 0, 0)),
                pl.BlockSpec((2, 1, cont_len, HEAD_SIZE), lambda s, i, *_: (0, s, 0, 0)),
            ],
            out_specs=pl.BlockSpec((1, block, width), lambda s, i, *_: (s, i, 0)),
        ),
        compiler_params=pltpu.CompilerParams(vmem_limit_bytes=48 * 1024 * 1024),
        name="attend",
    )(lengths, offsets, base, page_owner[None, :], queries, own_prompt, own_cont)


def solution(mesh):
    samples, ctx = mesh.shape["sample"], mesh.shape["ctx"]

    def local(queries, prompt, cont, page_owner, lengths, offsets):
        own_prompt, own_cont = gather(prompt, cont, samples, ctx)
        base = (lax.axis_index("sample") * queries.shape[0]).reshape(1)
        return attend(queries, own_prompt, own_cont, page_owner, lengths, offsets, base)

    in_specs = (
        P("sample", None, "ctx"),
        P(None, "ctx", "sample"),
        P(None, "sample", "ctx", None),
        P(),
        P(),
        P(),
    )
    out_specs = P("sample", None, "ctx")
    return jax.shard_map(local, mesh=mesh, in_specs=in_specs, out_specs=out_specs, check_vma=False)
```

```python
import functools
import math

import jax
import jax.numpy as jnp
from jax import lax
from jax.experimental import pallas as pl
from jax.experimental.pallas import tpu as pltpu
from jax.sharding import PartitionSpec as P

KEY_VALUE_HEADS = 8
HEAD_SIZE = 128
MESH = pl.DeviceIdType.MESH

neg_large = -1e30
query_block = 128


def gather_kernel(
    samples,
    ctx,
    prompt_ref,
    cont_ref,
    own_prompt,
    own_cont,
    swapped,
    swap_sems,
    cross_sems,
    relay_send,
    relay_recv,
    prompt_send,
    prompt_recv,
    cont_send,
    cont_forward,
    cont_recv,
):
    groups = KEY_VALUE_HEADS
    copies = ctx // groups
    shard_heads = prompt_ref.shape[2] // HEAD_SIZE
    sample = lax.axis_index("sample")
    me = lax.axis_index("ctx")
    group = me // copies
    rank = lax.rem(me, copies)

    siblings = [group * copies + lax.rem(rank + k, copies) for k in range(1, copies)]

    barrier = pltpu.get_barrier_semaphore()
    count = 0
    for ds in range(samples):
        for j in range(groups):
            if ds == 0 and j == 0:
                continue
            peer = lax.rem(group + j, groups) * copies + rank
            pl.semaphore_signal(
                barrier,
                inc=1,
                device_id=(lax.rem(sample + ds, samples), peer),
                device_id_type=MESH,
            )
            count += 1
    for sibling in siblings:
        pl.semaphore_signal(
            barrier, inc=1, device_id=(sample, sibling), device_id_type=MESH
        )
        count += 1
    pl.semaphore_wait(barrier, count)

    def head_columns(head):
        return pl.ds(pl.multiple_of(head * HEAD_SIZE, HEAD_SIZE), HEAD_SIZE)

    sends = []

    def send(src, dst, send_sem, recv_sem, device_id):
        copy = pltpu.make_async_remote_copy(
            src_ref=src,
            dst_ref=dst,
            send_sem=send_sem,
            recv_sem=recv_sem,
            device_id=device_id,
            device_id_type=MESH,
        )
        copy.start()
        return copy

    own_piece = cont_ref.at[:, :, :, head_columns(group)]
    pltpu.make_async_copy(own_piece, own_cont.at[:, :, group, rank], cont_recv.at[me]).start()

    def wait_slot(buffer, sem):
        pltpu.make_async_copy(buffer, buffer, sem).wait()

    def start_unless(mine, copy, src, dst, recv_sem):
        @pl.when(mine)
        def _():
            pltpu.make_async_copy(src, dst, recv_sem).start()

        @pl.when(jnp.logical_not(mine))
        def _():
            copy.start()

        sends.append((copy, jnp.logical_not(mine)))

    def send_cont(j):
        target = lax.rem(group + j, groups)
        sends.append(
            send(
                cont_ref.at[:, :, :, head_columns(target)],
                own_cont.at[:, :, group, rank],
                cont_send.at[j],
                cont_recv.at[me],
                (sample, target * copies + rank),
            )
        )

    def send_prompt(kind, part, ds, source, shard):
        local = lax.rem(part + group, shard_heads)
        head = shard * shard_heads + local
        target_sample = lax.rem(sample + ds, samples)
        index = part * samples + ds + (shard_heads * samples if kind == 1 else 0)
        if kind is None:
            src = source.at[:, :, head_columns(local)]
            dst = own_prompt.at[:, group, rank]
        else:
            src = source.at[:, head_columns(local)]
            dst = own_prompt.at[kind, group, rank]
        copy = pltpu.make_async_remote_copy(
            src_ref=src,
            dst_ref=dst,
            send_sem=prompt_send.at[index],
            recv_sem=prompt_recv.at[group],
            device_id=(target_sample, head * copies + rank),
            device_id_type=MESH,
        )
        if ds == 0:
            start_unless(head == group, copy, src, dst, prompt_recv.at[group])
        else:
            copy.start()
            sends.append(copy)

    def relay(buffer, index):
        for k, sibling in enumerate(siblings):
            sends.append(
                send(
                    buffer,
                    buffer,
                    relay_send.at[index, k],
                    relay_recv.at[index, rank],
                    (sample, sibling),
                )
            )

    half = groups // 2
    order = sorted(range(1, groups), key=lambda j: (abs(j - half), j))
    early, late = order[: half - 1], order[half - 1 :]
    if samples == 2:
        other = 1 - sample
        swap = send(prompt_ref.at[1], swapped, swap_sems.at[0], swap_sems.at[1], (other, me))
        for part in range(shard_heads):
            send_prompt(0, part, 0, prompt_ref.at[0], sample)
        for j in early:
            send_cont(j)
        swap.wait_recv()
        for part in range(shard_heads):
            send_prompt(1, part, 0, swapped, other)
        for j in late:
            send_cont(j)
    else:
        for part in range(shard_heads):
            for ds in range(samples):
                send_prompt(None, part, ds, prompt_ref, sample)
        for j in order:
            send_cont(j)

    for k, sibling in enumerate(siblings):
        sends.append(
            send(
                own_piece,
                own_cont.at[:, :, group, rank],
                cont_forward.at[0, k],
                cont_recv.at[me],
                (sample, sibling),
            )
        )
    wait_slot(own_cont.at[:, :, group, rank], cont_recv.at[me])

    def forward_cont(j):
        source = lax.rem(group + groups - j, groups)
        slot = source * copies + rank
        wait_slot(own_cont.at[:, :, source, rank], cont_recv.at[slot])
        for k, sibling in enumerate(siblings):
            sends.append(
                send(
                    own_cont.at[:, :, source, rank],
                    own_cont.at[:, :, source, rank],
                    cont_forward.at[j, k],
                    cont_recv.at[slot],
                    (sample, sibling),
                )
            )

    if samples == 2:
        direct = lax.rem(group // shard_heads + sample, 2)
        arrived = own_prompt.at[direct, :, rank]
        crossed = own_prompt.at[1 - direct, :, rank]
        for j in range(groups):
            wait_slot(own_prompt.at[direct, j, rank], prompt_recv.at[j])
        sends.append(send(arrived, arrived, cross_sems.at[0], cross_sems.at[1], (other, me)))
        relay(arrived, 0)
        for j in early:
            forward_cont(j)
        wait_slot(crossed, cross_sems.at[1])
        relay(crossed, 1)
        for j in late:
            forward_cont(j)
        swap.wait_send()
    else:
        for j in range(groups):
            wait_slot(own_prompt.at[:, j, rank], prompt_recv.at[j])
        relay(own_prompt.at[:, :, rank], 0)
        for j in order:
            forward_cont(j)

    for k in range(1, copies):
        peer = lax.rem(rank + copies - k, copies)
        if samples == 2:
            wait_slot(own_prompt.at[direct, :, peer], relay_recv.at[0, peer])
            wait_slot(own_prompt.at[1 - direct, :, peer], relay_recv.at[1, peer])
        else:
            wait_slot(own_prompt.at[:, :, peer], relay_recv.at[0, peer])
        for j in range(groups):
            wait_slot(own_cont.at[:, :, j, peer], cont_recv.at[j * copies + peer])

    for item in sends:
        if isinstance(item, tuple):
            copy, started = item

            @pl.when(started)
            def _():
                copy.wait_send()
        else:
            item.wait_send()


def gather(prompt, cont, samples, ctx):
    groups = KEY_VALUE_HEADS
    copies = ctx // groups
    prompt_rows = prompt.shape[1]
    here, cont_rows = cont.shape[1:3]
    shard_heads = prompt.shape[2] // HEAD_SIZE
    forwards = max(copies - 1, 1)
    anywhere = pl.BlockSpec(memory_space=pl.ANY)
    own_prompt, own_cont = pl.pallas_call(
        functools.partial(gather_kernel, samples, ctx),
        out_shape=(
            jax.ShapeDtypeStruct((2, groups, copies, prompt_rows, HEAD_SIZE), prompt.dtype),
            jax.ShapeDtypeStruct((2, here, groups, copies, cont_rows, HEAD_SIZE), cont.dtype),
        ),
        in_specs=[anywhere, anywhere],
        out_specs=(anywhere, anywhere),
        scratch_shapes=[
            pltpu.VMEM(prompt.shape[1:], prompt.dtype),
            pltpu.SemaphoreType.DMA((2,)),
            pltpu.SemaphoreType.DMA((2,)),
            pltpu.SemaphoreType.DMA((2, forwards)),
            pltpu.SemaphoreType.DMA((2, copies)),
            pltpu.SemaphoreType.DMA((2 * shard_heads * samples,)),
            pltpu.SemaphoreType.DMA((groups,)),
            pltpu.SemaphoreType.DMA((groups,)),
            pltpu.SemaphoreType.DMA((groups, forwards)),
            pltpu.SemaphoreType.DMA((ctx,)),
        ],
        compiler_params=pltpu.CompilerParams(collective_id=0, has_side_effects=True),
        name="gather_heads",
    )(prompt, cont)
    own_prompt = own_prompt.reshape(2, ctx * prompt_rows, HEAD_SIZE)
    own_cont = own_cont.reshape(2, here, ctx * cont_rows, HEAD_SIZE)
    return own_prompt, own_cont


def attend_kernel(block, lengths, offsets, base, owner_ref, q_ref, prompt_ref, cont_ref, out_ref):
    heads = q_ref.shape[2] // HEAD_SIZE
    prompt_len = prompt_ref.shape[1]
    blocks = cont_ref.shape[2] // block
    sample = base[0] + pl.program_id(0)
    step = pl.program_id(1)
    length = lengths[sample]
    factor = HEAD_SIZE ** -0.5 * math.log2(math.e)
    contract_last = (((1,), (1,)), ((), ()))

    live = step * block < length

    @pl.when(jnp.logical_not(live))
    def _():
        out_ref[...] = jnp.zeros_like(out_ref)

    def with_ones(values):
        return jnp.concatenate([values, jnp.ones_like(values)], axis=1)

    for i in range(blocks):

        @pl.when(live & (step == i))
        def _():
            extent = (i + 1) * block
            q = jnp.concatenate(
                [q_ref[0, :, h * HEAD_SIZE : (h + 1) * HEAD_SIZE] for h in range(heads)], axis=0
            )
            owner = owner_ref[...]
            position = lax.broadcasted_iota(jnp.int32, (1, prompt_len), 1)
            seen = ((owner == 0) | (owner == sample + 1)) & (position < offsets[sample])
            bias = jnp.where(seen, 0.0, neg_large)
            first = lax.dot_general(
                q, prompt_ref[0], contract_last, preferred_element_type=jnp.float32
            )
            first = first + bias
            second = lax.dot_general(
                q, cont_ref[0, 0, :extent], contract_last, preferred_element_type=jnp.float32
            )
            row = lax.broadcasted_iota(jnp.int32, (block, block), 0)
            col = lax.broadcasted_iota(jnp.int32, (block, block), 1)
            causal = jnp.where(col <= row, 0.0, neg_large)
            causal = jnp.concatenate([causal] * heads, axis=0)
            diagonal = second[:, i * block :] + causal
            if i:
                second = jnp.concatenate([second[:, : i * block], diagonal], axis=1)
            else:
                second = diagonal
            row_max = jnp.maximum(
                jnp.max(first, axis=1, keepdims=True), jnp.max(second, axis=1, keepdims=True)
            )
            first = jnp.exp2((first - row_max) * factor).astype(jnp.bfloat16)
            second = jnp.exp2((second - row_max) * factor).astype(jnp.bfloat16)
            total = jnp.dot(
                first, with_ones(prompt_ref[1]), preferred_element_type=jnp.float32
            ) + jnp.dot(
                second, with_ones(cont_ref[1, 0, :extent]), preferred_element_type=jnp.float32
            )
            mixed = total[:, :HEAD_SIZE] / total[:, HEAD_SIZE:]
            place = i * block + lax.broadcasted_iota(jnp.int32, (block, HEAD_SIZE), 0)
            for h in range(heads):
                out_ref[0, :, h * HEAD_SIZE : (h + 1) * HEAD_SIZE] = jnp.where(
                    place < length, mixed[h * block : (h + 1) * block], 0.0
                ).astype(out_ref.dtype)


def attend(queries, own_prompt, own_cont, page_owner, lengths, offsets, base):
    here, cont_len, width = queries.shape
    prompt_len = own_prompt.shape[1]
    block = math.gcd(query_block, cont_len)
    return pl.pallas_call(
        functools.partial(attend_kernel, block),
        out_shape=jax.ShapeDtypeStruct(queries.shape, queries.dtype),
        grid_spec=pltpu.PrefetchScalarGridSpec(
            num_scalar_prefetch=3,
            grid=(here, cont_len // block),
            in_specs=[
                pl.BlockSpec((1, prompt_len), lambda s, i, *_: (0, 0)),
                pl.BlockSpec((1, block, width), lambda s, i, *_: (s, i, 0)),
                pl.BlockSpec((2, prompt_len, HEAD_SIZE), lambda s, i, *_: (0, 0, 0)),
                pl.BlockSpec((2, 1, cont_len, HEAD_SIZE), lambda s, i, *_: (0, s, 0, 0)),
            ],
            out_specs=pl.BlockSpec((1, block, width), lambda s, i, *_: (s, i, 0)),
        ),
        compiler_params=pltpu.CompilerParams(vmem_limit_bytes=60 * 1024 * 1024),
        name="attend",
    )(lengths, offsets, base, page_owner[None, :], queries, own_prompt, own_cont)


def solution(mesh):
    samples, ctx = mesh.shape["sample"], mesh.shape["ctx"]

    def local(queries, prompt, cont, page_owner, lengths, offsets):
        own_prompt, own_cont = gather(prompt, cont, samples, ctx)
        base = (lax.axis_index("sample") * queries.shape[0]).reshape(1)
        return attend(queries, own_prompt, own_cont, page_owner, lengths, offsets, base)

    in_specs = (
        P("sample", None, "ctx"),
        P(None, "ctx", "sample"),
        P(None, "sample", "ctx", None),
        P(),
        P(),
        P(),
    )
    out_specs = P("sample", None, "ctx")
    return jax.shard_map(local, mesh=mesh, in_specs=in_specs, out_specs=out_specs, check_vma=False)
```

```python
import functools
import math

import jax
import jax.numpy as jnp
from jax import lax
from jax.experimental import pallas as pl
from jax.experimental.pallas import tpu as pltpu
from jax.sharding import PartitionSpec as P

KEY_VALUE_HEADS = 8
HEAD_SIZE = 128
MESH = pl.DeviceIdType.MESH

neg_large = -1e30
query_block = 256
batches = 2


def gather_kernel(
    samples,
    ctx,
    prompt_ref,
    cont_ref,
    own_prompt,
    own_cont,
    swapped,
    swap_sems,
    cross_sems,
    relay_send,
    relay_recv,
    prompt_send,
    prompt_recv,
    cont_send,
    cont_forward,
    cont_recv,
):
    groups = KEY_VALUE_HEADS
    copies = ctx // groups
    shard_heads = prompt_ref.shape[2] // HEAD_SIZE
    sample = lax.axis_index("sample")
    me = lax.axis_index("ctx")
    group = me // copies
    rank = lax.rem(me, copies)

    siblings = [group * copies + lax.rem(rank + k, copies) for k in range(1, copies)]

    barrier = pltpu.get_barrier_semaphore()
    count = 0
    for ds in range(samples):
        for j in range(groups):
            if ds == 0 and j == 0:
                continue
            peer = lax.rem(group + j, groups) * copies + rank
            pl.semaphore_signal(
                barrier,
                inc=1,
                device_id=(lax.rem(sample + ds, samples), peer),
                device_id_type=MESH,
            )
            count += 1
    for sibling in siblings:
        pl.semaphore_signal(
            barrier, inc=1, device_id=(sample, sibling), device_id_type=MESH
        )
        count += 1
    pl.semaphore_wait(barrier, count)

    def head_columns(head):
        return pl.ds(pl.multiple_of(head * HEAD_SIZE, HEAD_SIZE), HEAD_SIZE)

    sends = []

    def send(src, dst, send_sem, recv_sem, device_id):
        copy = pltpu.make_async_remote_copy(
            src_ref=src,
            dst_ref=dst,
            send_sem=send_sem,
            recv_sem=recv_sem,
            device_id=device_id,
            device_id_type=MESH,
        )
        copy.start()
        return copy

    own_piece = cont_ref.at[:, :, :, head_columns(group)]
    pltpu.make_async_copy(own_piece, own_cont.at[:, :, group, rank], cont_recv.at[me]).start()

    def wait_slot(buffer, sem):
        pltpu.make_async_copy(buffer, buffer, sem).wait()

    def start_unless(mine, copy, src, dst, recv_sem):
        @pl.when(mine)
        def _():
            pltpu.make_async_copy(src, dst, recv_sem).start()

        @pl.when(jnp.logical_not(mine))
        def _():
            copy.start()

        sends.append((copy, jnp.logical_not(mine)))

    def send_cont(j):
        target = lax.rem(group + j, groups)
        sends.append(
            send(
                cont_ref.at[:, :, :, head_columns(target)],
                own_cont.at[:, :, group, rank],
                cont_send.at[j],
                cont_recv.at[me],
                (sample, target * copies + rank),
            )
        )

    def send_prompt(kind, part, ds, source, shard):
        local = lax.rem(part + group, shard_heads)
        head = shard * shard_heads + local
        target_sample = lax.rem(sample + ds, samples)
        index = part * samples + ds + (shard_heads * samples if kind == 1 else 0)
        if kind is None:
            src = source.at[:, :, head_columns(local)]
            dst = own_prompt.at[:, group, rank]
        else:
            src = source.at[:, head_columns(local)]
            dst = own_prompt.at[kind, group, rank]
        copy = pltpu.make_async_remote_copy(
            src_ref=src,
            dst_ref=dst,
            send_sem=prompt_send.at[index],
            recv_sem=prompt_recv.at[group],
            device_id=(target_sample, head * copies + rank),
            device_id_type=MESH,
        )
        if ds == 0:
            start_unless(head == group, copy, src, dst, prompt_recv.at[group])
        else:
            copy.start()
            sends.append(copy)

    size = groups // batches

    def batch(b):
        return lax.rem(group // size + b, batches)

    def batch_ref(kind, b, at):
        return own_prompt.at[kind, pl.ds(batch(b) * size, size), at]

    def relay(buffer, index, b):
        for k, sibling in enumerate(siblings):
            sends.append(
                send(
                    buffer,
                    buffer,
                    relay_send.at[index, b, k],
                    relay_recv.at[index, batch(b), rank],
                    (sample, sibling),
                )
            )

    half = groups // 2
    order = sorted(range(1, groups), key=lambda j: (abs(j - half), j))
    early, late = order[: half - 1], order[half - 1 :]
    if samples == 2:
        other = 1 - sample
        swap = send(prompt_ref.at[1], swapped, swap_sems.at[0], swap_sems.at[1], (other, me))
        for part in range(shard_heads):
            send_prompt(0, part, 0, prompt_ref.at[0], sample)
        for j in early:
            send_cont(j)
        swap.wait_recv()
        for part in range(shard_heads):
            send_prompt(1, part, 0, swapped, other)
        for j in late:
            send_cont(j)
    else:
        for part in range(shard_heads):
            for ds in range(samples):
                send_prompt(None, part, ds, prompt_ref, sample)
        for j in order:
            send_cont(j)

    for k, sibling in enumerate(siblings):
        sends.append(
            send(
                own_piece,
                own_cont.at[:, :, group, rank],
                cont_forward.at[0, k],
                cont_recv.at[me],
                (sample, sibling),
            )
        )
    wait_slot(own_cont.at[:, :, group, rank], cont_recv.at[me])

    def forward_cont(j):
        source = lax.rem(group + groups - j, groups)
        slot = source * copies + rank
        wait_slot(own_cont.at[:, :, source, rank], cont_recv.at[slot])
        for k, sibling in enumerate(siblings):
            sends.append(
                send(
                    own_cont.at[:, :, source, rank],
                    own_cont.at[:, :, source, rank],
                    cont_forward.at[j, k],
                    cont_recv.at[slot],
                    (sample, sibling),
                )
            )

    if samples == 2:
        direct = lax.rem(group // shard_heads + sample, 2)
        for b in range(batches):
            for j in range(size):
                source = batch(b) * size + j
                wait_slot(own_prompt.at[direct, source, rank], prompt_recv.at[source])
            arrived = batch_ref(direct, b, rank)
            sends.append(
                send(
                    arrived,
                    arrived,
                    cross_sems.at[0, b],
                    cross_sems.at[1, batch(b)],
                    (other, me),
                )
            )
            relay(arrived, 0, b)
        for j in early:
            forward_cont(j)
        for b in range(batches):
            crossed = batch_ref(1 - direct, b, rank)
            wait_slot(crossed, cross_sems.at[1, batch(b)])
            relay(crossed, 1, b)
        for j in late:
            forward_cont(j)
        swap.wait_send()
    else:
        for j in range(groups):
            wait_slot(own_prompt.at[:, j, rank], prompt_recv.at[j])
        for b in range(batches):
            relay(own_prompt.at[:, pl.ds(batch(b) * size, size), rank], 0, b)
        for j in order:
            forward_cont(j)

    for k in range(1, copies):
        peer = lax.rem(rank + copies - k, copies)
        for b in range(batches):
            rows = pl.ds(b * size, size)
            if samples == 2:
                wait_slot(own_prompt.at[direct, rows, peer], relay_recv.at[0, b, peer])
                wait_slot(own_prompt.at[1 - direct, rows, peer], relay_recv.at[1, b, peer])
            else:
                wait_slot(own_prompt.at[:, rows, peer], relay_recv.at[0, b, peer])
        for j in range(groups):
            wait_slot(own_cont.at[:, :, j, peer], cont_recv.at[j * copies + peer])

    for item in sends:
        if isinstance(item, tuple):
            copy, started = item

            @pl.when(started)
            def _():
                copy.wait_send()
        else:
            item.wait_send()


def gather(prompt, cont, samples, ctx):
    groups = KEY_VALUE_HEADS
    copies = ctx // groups
    prompt_rows = prompt.shape[1]
    here, cont_rows = cont.shape[1:3]
    shard_heads = prompt.shape[2] // HEAD_SIZE
    forwards = max(copies - 1, 1)
    anywhere = pl.BlockSpec(memory_space=pl.ANY)
    own_prompt, own_cont = pl.pallas_call(
        functools.partial(gather_kernel, samples, ctx),
        out_shape=(
            jax.ShapeDtypeStruct((2, groups, copies, prompt_rows, HEAD_SIZE), prompt.dtype),
            jax.ShapeDtypeStruct((2, here, groups, copies, cont_rows, HEAD_SIZE), cont.dtype),
        ),
        in_specs=[anywhere, anywhere],
        out_specs=(anywhere, anywhere),
        scratch_shapes=[
            pltpu.VMEM(prompt.shape[1:], prompt.dtype),
            pltpu.SemaphoreType.DMA((2,)),
            pltpu.SemaphoreType.DMA((2, batches)),
            pltpu.SemaphoreType.DMA((2, batches, forwards)),
            pltpu.SemaphoreType.DMA((2, batches, copies)),
            pltpu.SemaphoreType.DMA((2 * shard_heads * samples,)),
            pltpu.SemaphoreType.DMA((groups,)),
            pltpu.SemaphoreType.DMA((groups,)),
            pltpu.SemaphoreType.DMA((groups, forwards)),
            pltpu.SemaphoreType.DMA((ctx,)),
        ],
        compiler_params=pltpu.CompilerParams(collective_id=0, has_side_effects=True),
        name="gather_heads",
    )(prompt, cont)
    own_prompt = own_prompt.reshape(2, ctx * prompt_rows, HEAD_SIZE)
    own_cont = own_cont.reshape(2, here, ctx * cont_rows, HEAD_SIZE)
    return own_prompt, own_cont


def attend_kernel(block, lengths, offsets, base, owner_ref, q_ref, prompt_ref, cont_ref, out_ref):
    heads = q_ref.shape[2] // HEAD_SIZE
    prompt_len = prompt_ref.shape[1]
    blocks = cont_ref.shape[2] // block
    sample = base[0] + pl.program_id(0)
    step = pl.program_id(1)
    length = lengths[sample]
    factor = HEAD_SIZE ** -0.5 * math.log2(math.e)
    contract_last = (((1,), (1,)), ((), ()))

    live = step * block < length

    @pl.when(jnp.logical_not(live))
    def _():
        out_ref[...] = jnp.zeros_like(out_ref)

    def with_ones(values):
        return jnp.concatenate([values, jnp.ones_like(values)], axis=1)

    for i in range(blocks):

        @pl.when(live & (step == i))
        def _():
            extent = (i + 1) * block
            owner = owner_ref[...]
            position = lax.broadcasted_iota(jnp.int32, (1, prompt_len), 1)
            seen = ((owner == 0) | (owner == sample + 1)) & (position < offsets[sample])
            bias = jnp.where(seen, 0.0, neg_large)
            row = lax.broadcasted_iota(jnp.int32, (block, block), 0)
            col = lax.broadcasted_iota(jnp.int32, (block, block), 1)
            causal = jnp.where(col <= row, 0.0, neg_large)
            place = i * block + lax.broadcasted_iota(jnp.int32, (block, HEAD_SIZE), 0)
            prompt_values = with_ones(prompt_ref[1])
            cont_values = with_ones(cont_ref[1, 0, :extent])

            def scores(h):
                q = q_ref[0, :, h * HEAD_SIZE : (h + 1) * HEAD_SIZE]
                first = lax.dot_general(
                    q, prompt_ref[0], contract_last, preferred_element_type=jnp.float32
                )
                second = lax.dot_general(
                    q, cont_ref[0, 0, :extent], contract_last, preferred_element_type=jnp.float32
                )
                first = first + bias
                diagonal = second[:, i * block :] + causal
                if i:
                    second = jnp.concatenate([second[:, : i * block], diagonal], axis=1)
                else:
                    second = diagonal
                return first, second

            def finish(h, first, second):
                row_max = jnp.maximum(
                    jnp.max(first, axis=1, keepdims=True), jnp.max(second, axis=1, keepdims=True)
                )
                first = jnp.exp2((first - row_max) * factor).astype(jnp.bfloat16)
                second = jnp.exp2((second - row_max) * factor).astype(jnp.bfloat16)
                total = jnp.dot(first, prompt_values, preferred_element_type=jnp.float32) + jnp.dot(
                    second, cont_values, preferred_element_type=jnp.float32
                )
                mixed = total[:, :HEAD_SIZE] / total[:, HEAD_SIZE:]
                out_ref[0, :, h * HEAD_SIZE : (h + 1) * HEAD_SIZE] = jnp.where(
                    place < length, mixed, 0.0
                ).astype(out_ref.dtype)

            held = scores(0)
            for h in range(heads):
                following = scores(h + 1) if h + 1 < heads else None
                finish(h, *held)
                held = following


def attend(queries, own_prompt, own_cont, page_owner, lengths, offsets, base):
    here, cont_len, width = queries.shape
    prompt_len = own_prompt.shape[1]
    block = math.gcd(query_block, cont_len)
    return pl.pallas_call(
        functools.partial(attend_kernel, block),
        out_shape=jax.ShapeDtypeStruct(queries.shape, queries.dtype),
        grid_spec=pltpu.PrefetchScalarGridSpec(
            num_scalar_prefetch=3,
            grid=(here, cont_len // block),
            in_specs=[
                pl.BlockSpec((1, prompt_len), lambda s, i, *_: (0, 0)),
                pl.BlockSpec((1, block, width), lambda s, i, *_: (s, i, 0)),
                pl.BlockSpec((2, prompt_len, HEAD_SIZE), lambda s, i, *_: (0, 0, 0)),
                pl.BlockSpec((2, 1, cont_len, HEAD_SIZE), lambda s, i, *_: (0, s, 0, 0)),
            ],
            out_specs=pl.BlockSpec((1, block, width), lambda s, i, *_: (s, i, 0)),
        ),
        compiler_params=pltpu.CompilerParams(vmem_limit_bytes=60 * 1024 * 1024),
        name="attend",
    )(lengths, offsets, base, page_owner[None, :], queries, own_prompt, own_cont)


def solution(mesh):
    samples, ctx = mesh.shape["sample"], mesh.shape["ctx"]

    def local(queries, prompt, cont, page_owner, lengths, offsets):
        own_prompt, own_cont = gather(prompt, cont, samples, ctx)
        base = (lax.axis_index("sample") * queries.shape[0]).reshape(1)
        return attend(queries, own_prompt, own_cont, page_owner, lengths, offsets, base)

    in_specs = (
        P("sample", None, "ctx"),
        P(None, "ctx", "sample"),
        P(None, "sample", "ctx", None),
        P(),
        P(),
        P(),
    )
    out_specs = P("sample", None, "ctx")
    return jax.shard_map(local, mesh=mesh, in_specs=in_specs, out_specs=out_specs, check_vma=False)
```

```python
import functools
import math

import jax
import jax.numpy as jnp
from jax import lax
from jax.experimental import pallas as pl
from jax.experimental.pallas import tpu as pltpu
from jax.sharding import PartitionSpec as P

KEY_VALUE_HEADS = 8
HEAD_SIZE = 128
MESH = pl.DeviceIdType.MESH

neg_large = -1e30
query_block = 256
batches = 2


def gather_kernel(
    samples,
    ctx,
    prompt_ref,
    cont_ref,
    own_prompt,
    own_cont,
    swapped,
    swap_sems,
    cross_sems,
    relay_send,
    relay_recv,
    prompt_send,
    prompt_recv,
    cont_send,
    cont_forward,
    cont_recv,
):
    groups = KEY_VALUE_HEADS
    copies = ctx // groups
    shard_heads = prompt_ref.shape[2] // HEAD_SIZE
    sample = lax.axis_index("sample")
    me = lax.axis_index("ctx")
    group = me // copies
    rank = lax.rem(me, copies)

    siblings = [group * copies + lax.rem(rank + k, copies) for k in range(1, copies)]

    barrier = pltpu.get_barrier_semaphore()
    count = 0
    for ds in range(samples):
        for j in range(groups):
            if (ds == 0 and j == 0) or (samples == 2 and ds == 1 and j > 0):
                continue
            peer = lax.rem(group + j, groups) * copies + rank
            pl.semaphore_signal(
                barrier,
                inc=1,
                device_id=(lax.rem(sample + ds, samples), peer),
                device_id_type=MESH,
            )
            count += 1
    for sibling in siblings:
        pl.semaphore_signal(
            barrier, inc=1, device_id=(sample, sibling), device_id_type=MESH
        )
        count += 1
    pl.semaphore_wait(barrier, count)

    def head_columns(head):
        return pl.ds(pl.multiple_of(head * HEAD_SIZE, HEAD_SIZE), HEAD_SIZE)

    sends = []

    def send(src, dst, send_sem, recv_sem, device_id):
        copy = pltpu.make_async_remote_copy(
            src_ref=src,
            dst_ref=dst,
            send_sem=send_sem,
            recv_sem=recv_sem,
            device_id=device_id,
            device_id_type=MESH,
        )
        copy.start()
        return copy

    own_piece = cont_ref.at[:, :, :, head_columns(group)]
    pltpu.make_async_copy(own_piece, own_cont.at[:, :, group, rank], cont_recv.at[me]).start()

    def wait_slot(buffer, sem):
        pltpu.make_async_copy(buffer, buffer, sem).wait()

    def start_unless(mine, copy, src, dst, recv_sem):
        @pl.when(mine)
        def _():
            pltpu.make_async_copy(src, dst, recv_sem).start()

        @pl.when(jnp.logical_not(mine))
        def _():
            copy.start()

        sends.append((copy, jnp.logical_not(mine)))

    def send_cont(j):
        target = lax.rem(group + j, groups)
        sends.append(
            send(
                cont_ref.at[:, :, :, head_columns(target)],
                own_cont.at[:, :, group, rank],
                cont_send.at[j],
                cont_recv.at[me],
                (sample, target * copies + rank),
            )
        )

    def send_prompt(kind, part, ds, source, shard):
        local = lax.rem(part + group, shard_heads)
        head = shard * shard_heads + local
        target_sample = lax.rem(sample + ds, samples)
        index = part * samples + ds + (shard_heads * samples if kind == 1 else 0)
        if kind is None:
            src = source.at[:, :, head_columns(local)]
            dst = own_prompt.at[:, group, rank]
        else:
            src = source.at[:, head_columns(local)]
            dst = own_prompt.at[kind, group, rank]
        copy = pltpu.make_async_remote_copy(
            src_ref=src,
            dst_ref=dst,
            send_sem=prompt_send.at[index],
            recv_sem=prompt_recv.at[group],
            device_id=(target_sample, head * copies + rank),
            device_id_type=MESH,
        )
        if ds == 0:
            start_unless(head == group, copy, src, dst, prompt_recv.at[group])
        else:
            copy.start()
            sends.append(copy)

    size = groups // batches

    def batch(b):
        return lax.rem(group // size + b, batches)

    def batch_ref(kind, b, at):
        return own_prompt.at[kind, pl.ds(batch(b) * size, size), at]

    def relay(buffer, index, b):
        for k, sibling in enumerate(siblings):
            sends.append(
                send(
                    buffer,
                    buffer,
                    relay_send.at[index, b, k],
                    relay_recv.at[index, batch(b), rank],
                    (sample, sibling),
                )
            )

    half = groups // 2
    order = sorted(range(1, groups), key=lambda j: (abs(j - half), j))
    early, late = order[: half - 1], order[half - 1 :]
    if samples == 2:
        other = 1 - sample
        swap = send(prompt_ref.at[1], swapped, swap_sems.at[0], swap_sems.at[1], (other, me))
        for part in range(shard_heads):
            send_prompt(0, part, 0, prompt_ref.at[0], sample)
        for j in early:
            send_cont(j)
        swap.wait_recv()
        for part in range(shard_heads):
            send_prompt(1, part, 0, swapped, other)
        for j in late:
            send_cont(j)
    else:
        for part in range(shard_heads):
            for ds in range(samples):
                send_prompt(None, part, ds, prompt_ref, sample)
        for j in order:
            send_cont(j)

    for k, sibling in enumerate(siblings):
        sends.append(
            send(
                own_piece,
                own_cont.at[:, :, group, rank],
                cont_forward.at[0, k],
                cont_recv.at[me],
                (sample, sibling),
            )
        )
    wait_slot(own_cont.at[:, :, group, rank], cont_recv.at[me])

    def forward_cont(j):
        source = lax.rem(group + groups - j, groups)
        slot = source * copies + rank
        wait_slot(own_cont.at[:, :, source, rank], cont_recv.at[slot])
        for k, sibling in enumerate(siblings):
            sends.append(
                send(
                    own_cont.at[:, :, source, rank],
                    own_cont.at[:, :, source, rank],
                    cont_forward.at[j, k],
                    cont_recv.at[slot],
                    (sample, sibling),
                )
            )

    if samples == 2:
        direct = lax.rem(group // shard_heads + sample, 2)
        for b in range(batches):
            for j in range(size):
                source = batch(b) * size + j
                wait_slot(own_prompt.at[direct, source, rank], prompt_recv.at[source])
            arrived = batch_ref(direct, b, rank)
            sends.append(
                send(
                    arrived,
                    arrived,
                    cross_sems.at[0, b],
                    cross_sems.at[1, batch(b)],
                    (other, me),
                )
            )
            relay(arrived, 0, b)
        for j in early:
            forward_cont(j)
        for b in range(batches):
            crossed = batch_ref(1 - direct, b, rank)
            wait_slot(crossed, cross_sems.at[1, batch(b)])
            relay(crossed, 1, b)
        for j in late:
            forward_cont(j)
        swap.wait_send()
    else:
        for j in range(groups):
            wait_slot(own_prompt.at[:, j, rank], prompt_recv.at[j])
        for b in range(batches):
            relay(own_prompt.at[:, pl.ds(batch(b) * size, size), rank], 0, b)
        for j in order:
            forward_cont(j)

    for k in range(1, copies):
        peer = lax.rem(rank + copies - k, copies)
        for b in range(batches):
            rows = pl.ds(b * size, size)
            if samples == 2:
                wait_slot(own_prompt.at[direct, rows, peer], relay_recv.at[0, b, peer])
                wait_slot(own_prompt.at[1 - direct, rows, peer], relay_recv.at[1, b, peer])
            else:
                wait_slot(own_prompt.at[:, rows, peer], relay_recv.at[0, b, peer])
        for j in range(groups):
            wait_slot(own_cont.at[:, :, j, peer], cont_recv.at[j * copies + peer])

    for item in sends:
        if isinstance(item, tuple):
            copy, started = item

            @pl.when(started)
            def _():
                copy.wait_send()
        else:
            item.wait_send()


def gather(prompt, cont, samples, ctx):
    groups = KEY_VALUE_HEADS
    copies = ctx // groups
    prompt_rows = prompt.shape[1]
    here, cont_rows = cont.shape[1:3]
    shard_heads = prompt.shape[2] // HEAD_SIZE
    forwards = max(copies - 1, 1)
    anywhere = pl.BlockSpec(memory_space=pl.ANY)
    own_prompt, own_cont = pl.pallas_call(
        functools.partial(gather_kernel, samples, ctx),
        out_shape=(
            jax.ShapeDtypeStruct((2, groups, copies, prompt_rows, HEAD_SIZE), prompt.dtype),
            jax.ShapeDtypeStruct((2, here, groups, copies, cont_rows, HEAD_SIZE), cont.dtype),
        ),
        in_specs=[anywhere, anywhere],
        out_specs=(anywhere, anywhere),
        scratch_shapes=[
            pltpu.VMEM(prompt.shape[1:], prompt.dtype),
            pltpu.SemaphoreType.DMA((2,)),
            pltpu.SemaphoreType.DMA((2, batches)),
            pltpu.SemaphoreType.DMA((2, batches, forwards)),
            pltpu.SemaphoreType.DMA((2, batches, copies)),
            pltpu.SemaphoreType.DMA((2 * shard_heads * samples,)),
            pltpu.SemaphoreType.DMA((groups,)),
            pltpu.SemaphoreType.DMA((groups,)),
            pltpu.SemaphoreType.DMA((groups, forwards)),
            pltpu.SemaphoreType.DMA((ctx,)),
        ],
        compiler_params=pltpu.CompilerParams(collective_id=0, has_side_effects=True),
        name="gather_heads",
    )(prompt, cont)
    own_prompt = own_prompt.reshape(2, ctx * prompt_rows, HEAD_SIZE)
    own_cont = own_cont.reshape(2, here, ctx * cont_rows, HEAD_SIZE)
    return own_prompt, own_cont


def attend_kernel(block, lengths, offsets, base, owner_ref, q_ref, prompt_ref, cont_ref, out_ref):
    heads = q_ref.shape[2] // HEAD_SIZE
    prompt_len = prompt_ref.shape[1]
    blocks = cont_ref.shape[2] // block
    sample = base[0] + pl.program_id(0)
    step = pl.program_id(1)
    length = lengths[sample]
    factor = HEAD_SIZE ** -0.5 * math.log2(math.e)
    contract_last = (((1,), (1,)), ((), ()))

    live = step * block < length

    @pl.when(jnp.logical_not(live))
    def _():
        out_ref[...] = jnp.zeros_like(out_ref)

    def with_ones(values):
        return jnp.concatenate([values, jnp.ones_like(values)], axis=1)

    for i in range(blocks):

        @pl.when(live & (step == i))
        def _():
            extent = (i + 1) * block
            owner = owner_ref[...]
            position = lax.broadcasted_iota(jnp.int32, (1, prompt_len), 1)
            seen = ((owner == 0) | (owner == sample + 1)) & (position < offsets[sample])
            bias = jnp.where(seen, 0.0, neg_large)
            row = lax.broadcasted_iota(jnp.int32, (block, block), 0)
            col = lax.broadcasted_iota(jnp.int32, (block, block), 1)
            causal = jnp.where(col <= row, 0.0, neg_large)
            place = i * block + lax.broadcasted_iota(jnp.int32, (block, HEAD_SIZE), 0)
            prompt_values = with_ones(prompt_ref[1])
            cont_values = with_ones(cont_ref[1, 0, :extent])

            all_values = jnp.concatenate([prompt_values, cont_values], axis=0)

            def scores(h):
                q = q_ref[0, :, h * HEAD_SIZE : (h + 1) * HEAD_SIZE]
                first = lax.dot_general(
                    q, prompt_ref[0], contract_last, preferred_element_type=jnp.float32
                )
                second = lax.dot_general(
                    q, cont_ref[0, 0, :extent], contract_last, preferred_element_type=jnp.float32
                )
                first = first + bias
                diagonal = second[:, i * block :] + causal
                if i:
                    second = jnp.concatenate([second[:, : i * block], diagonal], axis=1)
                else:
                    second = diagonal
                return first, second

            def finish(h, first, second):
                row_max = jnp.maximum(
                    jnp.max(first, axis=1, keepdims=True), jnp.max(second, axis=1, keepdims=True)
                )
                first = jnp.exp2((first - row_max) * factor).astype(jnp.bfloat16)
                second = jnp.exp2((second - row_max) * factor).astype(jnp.bfloat16)
                total = jnp.dot(
                    jnp.concatenate([first, second], axis=1),
                    all_values,
                    preferred_element_type=jnp.float32,
                )
                mixed = total[:, :HEAD_SIZE] / total[:, HEAD_SIZE:]
                out_ref[0, :, h * HEAD_SIZE : (h + 1) * HEAD_SIZE] = jnp.where(
                    place < length, mixed, 0.0
                ).astype(out_ref.dtype)

            held = scores(0)
            for h in range(heads):
                following = scores(h + 1) if h + 1 < heads else None
                finish(h, *held)
                held = following


def attend(queries, own_prompt, own_cont, page_owner, lengths, offsets, base):
    here, cont_len, width = queries.shape
    prompt_len = own_prompt.shape[1]
    block = math.gcd(query_block, cont_len)
    return pl.pallas_call(
        functools.partial(attend_kernel, block),
        out_shape=jax.ShapeDtypeStruct(queries.shape, queries.dtype),
        grid_spec=pltpu.PrefetchScalarGridSpec(
            num_scalar_prefetch=3,
            grid=(here, cont_len // block),
            in_specs=[
                pl.BlockSpec((1, prompt_len), lambda s, i, *_: (0, 0)),
                pl.BlockSpec((1, block, width), lambda s, i, *_: (s, i, 0)),
                pl.BlockSpec((2, prompt_len, HEAD_SIZE), lambda s, i, *_: (0, 0, 0)),
                pl.BlockSpec((2, 1, cont_len, HEAD_SIZE), lambda s, i, *_: (0, s, 0, 0)),
            ],
            out_specs=pl.BlockSpec((1, block, width), lambda s, i, *_: (s, i, 0)),
        ),
        compiler_params=pltpu.CompilerParams(vmem_limit_bytes=60 * 1024 * 1024),
        name="attend",
    )(lengths, offsets, base, page_owner[None, :], queries, own_prompt, own_cont)


def solution(mesh):
    samples, ctx = mesh.shape["sample"], mesh.shape["ctx"]

    def local(queries, prompt, cont, page_owner, lengths, offsets):
        own_prompt, own_cont = gather(prompt, cont, samples, ctx)
        base = (lax.axis_index("sample") * queries.shape[0]).reshape(1)
        return attend(queries, own_prompt, own_cont, page_owner, lengths, offsets, base)

    in_specs = (
        P("sample", None, "ctx"),
        P(None, "ctx", "sample"),
        P(None, "sample", "ctx", None),
        P(),
        P(),
        P(),
    )
    out_specs = P("sample", None, "ctx")
    return jax.shard_map(local, mesh=mesh, in_specs=in_specs, out_specs=out_specs, check_vma=False)
```

```python
import functools
import math

import jax
import jax.numpy as jnp
from jax import lax
from jax.experimental import pallas as pl
from jax.experimental.pallas import tpu as pltpu
from jax.sharding import PartitionSpec as P

KEY_VALUE_HEADS = 8
HEAD_SIZE = 128
MESH = pl.DeviceIdType.MESH

neg_large = -1e30
query_block = 256
batches = 2


def gather_kernel(
    samples,
    ctx,
    prompt_ref,
    cont_ref,
    own_prompt,
    own_cont,
    swapped,
    swap_sems,
    relay_send,
    relay_recv,
    prompt_send,
    prompt_recv,
    cont_send,
    cont_forward,
    cont_recv,
):
    groups = KEY_VALUE_HEADS
    copies = ctx // groups
    shard_heads = prompt_ref.shape[2] // HEAD_SIZE
    sample = lax.axis_index("sample")
    me = lax.axis_index("ctx")
    group = me // copies
    rank = lax.rem(me, copies)

    siblings = [group * copies + lax.rem(rank + k, copies) for k in range(1, copies)]

    barrier = pltpu.get_barrier_semaphore()
    count = 0
    for ds in range(samples):
        for j in range(groups):
            if (ds == 0 and j == 0) or (samples == 2 and ds == 1 and j > 0):
                continue
            peer = lax.rem(group + j, groups) * copies + rank
            pl.semaphore_signal(
                barrier,
                inc=1,
                device_id=(lax.rem(sample + ds, samples), peer),
                device_id_type=MESH,
            )
            count += 1
    for sibling in siblings:
        pl.semaphore_signal(
            barrier, inc=1, device_id=(sample, sibling), device_id_type=MESH
        )
        count += 1
    pl.semaphore_wait(barrier, count)

    def head_columns(head):
        return pl.ds(pl.multiple_of(head * HEAD_SIZE, HEAD_SIZE), HEAD_SIZE)

    sends = []

    def send(src, dst, send_sem, recv_sem, device_id):
        copy = pltpu.make_async_remote_copy(
            src_ref=src,
            dst_ref=dst,
            send_sem=send_sem,
            recv_sem=recv_sem,
            device_id=device_id,
            device_id_type=MESH,
        )
        copy.start()
        return copy

    own_piece = cont_ref.at[:, :, :, head_columns(group)]
    pltpu.make_async_copy(own_piece, own_cont.at[:, :, group, rank], cont_recv.at[me]).start()

    def wait_slot(buffer, sem):
        pltpu.make_async_copy(buffer, buffer, sem).wait()

    def start_unless(mine, copy, src, dst, recv_sem):
        @pl.when(mine)
        def _():
            pltpu.make_async_copy(src, dst, recv_sem).start()

        @pl.when(jnp.logical_not(mine))
        def _():
            copy.start()

        sends.append((copy, jnp.logical_not(mine)))

    def send_cont(j):
        target = lax.rem(group + j, groups)
        sends.append(
            send(
                cont_ref.at[:, :, :, head_columns(target)],
                own_cont.at[:, :, group, rank],
                cont_send.at[j],
                cont_recv.at[me],
                (sample, target * copies + rank),
            )
        )

    def send_prompt(turn, part, ds, source, shard):
        local = lax.rem(part + group, shard_heads)
        head = shard * shard_heads + local
        target_sample = lax.rem(sample + ds, samples)
        index = part * samples + ds + (shard_heads * samples if turn == 1 else 0)
        src = source.at[:, :, head_columns(local)]
        dst = own_prompt.at[:, group, rank]
        copy = pltpu.make_async_remote_copy(
            src_ref=src,
            dst_ref=dst,
            send_sem=prompt_send.at[index],
            recv_sem=prompt_recv.at[group],
            device_id=(target_sample, head * copies + rank),
            device_id_type=MESH,
        )
        if ds == 0:
            start_unless(head == group, copy, src, dst, prompt_recv.at[group])
        else:
            copy.start()
            sends.append(copy)

    size = groups // batches

    def batch(b):
        return lax.rem(group // size + b, batches)

    def relay(buffer, b):
        for k, sibling in enumerate(siblings):
            sends.append(
                send(
                    buffer,
                    buffer,
                    relay_send.at[b, k],
                    relay_recv.at[batch(b), rank],
                    (sample, sibling),
                )
            )

    half = groups // 2
    order = sorted(range(1, groups), key=lambda j: (abs(j - half), j))
    early, late = order[: half - 1], order[half - 1 :]
    if samples == 2:
        other = 1 - sample
        swap = send(prompt_ref, swapped, swap_sems.at[0], swap_sems.at[1], (other, me))
        for part in range(shard_heads):
            send_prompt(0, part, 0, prompt_ref, sample)
        for j in early:
            send_cont(j)
        swap.wait_recv()
        for part in range(shard_heads):
            send_prompt(1, part, 0, swapped, other)
        for j in late:
            send_cont(j)
    else:
        for part in range(shard_heads):
            for ds in range(samples):
                send_prompt(0, part, ds, prompt_ref, sample)
        for j in order:
            send_cont(j)

    for k, sibling in enumerate(siblings):
        sends.append(
            send(
                own_piece,
                own_cont.at[:, :, group, rank],
                cont_forward.at[0, k],
                cont_recv.at[me],
                (sample, sibling),
            )
        )
    wait_slot(own_cont.at[:, :, group, rank], cont_recv.at[me])

    def forward_cont(j):
        source = lax.rem(group + groups - j, groups)
        slot = source * copies + rank
        wait_slot(own_cont.at[:, :, source, rank], cont_recv.at[slot])
        for k, sibling in enumerate(siblings):
            sends.append(
                send(
                    own_cont.at[:, :, source, rank],
                    own_cont.at[:, :, source, rank],
                    cont_forward.at[j, k],
                    cont_recv.at[slot],
                    (sample, sibling),
                )
            )

    for b in range(batches):
        for j in range(size):
            source = batch(b) * size + j
            wait_slot(own_prompt.at[:, source, rank], prompt_recv.at[source])
        relay(own_prompt.at[:, pl.ds(batch(b) * size, size), rank], b)
    for j in order:
        forward_cont(j)
    if samples == 2:
        swap.wait_send()

    for k in range(1, copies):
        peer = lax.rem(rank + copies - k, copies)
        for b in range(batches):
            rows = pl.ds(b * size, size)
            wait_slot(own_prompt.at[:, rows, peer], relay_recv.at[b, peer])
        for j in range(groups):
            wait_slot(own_cont.at[:, :, j, peer], cont_recv.at[j * copies + peer])

    for item in sends:
        if isinstance(item, tuple):
            copy, started = item

            @pl.when(started)
            def _():
                copy.wait_send()
        else:
            item.wait_send()


def gather(prompt, cont, samples, ctx):
    groups = KEY_VALUE_HEADS
    copies = ctx // groups
    prompt_rows = prompt.shape[1]
    here, cont_rows = cont.shape[1:3]
    shard_heads = prompt.shape[2] // HEAD_SIZE
    forwards = max(copies - 1, 1)
    anywhere = pl.BlockSpec(memory_space=pl.ANY)
    own_prompt, own_cont = pl.pallas_call(
        functools.partial(gather_kernel, samples, ctx),
        out_shape=(
            jax.ShapeDtypeStruct((2, groups, copies, prompt_rows, HEAD_SIZE), prompt.dtype),
            jax.ShapeDtypeStruct((2, here, groups, copies, cont_rows, HEAD_SIZE), cont.dtype),
        ),
        in_specs=[anywhere, anywhere],
        out_specs=(anywhere, anywhere),
        scratch_shapes=[
            pltpu.VMEM(prompt.shape, prompt.dtype),
            pltpu.SemaphoreType.DMA((2,)),
            pltpu.SemaphoreType.DMA((batches, forwards)),
            pltpu.SemaphoreType.DMA((batches, copies)),
            pltpu.SemaphoreType.DMA((2 * shard_heads * samples,)),
            pltpu.SemaphoreType.DMA((groups,)),
            pltpu.SemaphoreType.DMA((groups,)),
            pltpu.SemaphoreType.DMA((groups, forwards)),
            pltpu.SemaphoreType.DMA((ctx,)),
        ],
        compiler_params=pltpu.CompilerParams(collective_id=0, has_side_effects=True),
        name="gather_heads",
    )(prompt, cont)
    own_prompt = own_prompt.reshape(2, ctx * prompt_rows, HEAD_SIZE)
    own_cont = own_cont.reshape(2, here, ctx * cont_rows, HEAD_SIZE)
    return own_prompt, own_cont


def attend_kernel(block, lengths, offsets, base, owner_ref, q_ref, prompt_ref, cont_ref, out_ref):
    heads = q_ref.shape[2] // HEAD_SIZE
    prompt_len = prompt_ref.shape[1]
    blocks = cont_ref.shape[2] // block
    sample = base[0] + pl.program_id(0)
    step = pl.program_id(1)
    length = lengths[sample]
    factor = HEAD_SIZE ** -0.5 * math.log2(math.e)
    contract_last = (((1,), (1,)), ((), ()))

    live = step * block < length

    @pl.when(jnp.logical_not(live))
    def _():
        out_ref[...] = jnp.zeros_like(out_ref)

    def with_ones(values):
        return jnp.concatenate([values, jnp.ones_like(values)], axis=1)

    for i in range(blocks):

        @pl.when(live & (step == i))
        def _():
            extent = (i + 1) * block
            owner = owner_ref[...]
            position = lax.broadcasted_iota(jnp.int32, (1, prompt_len), 1)
            seen = ((owner == 0) | (owner == sample + 1)) & (position < offsets[sample])
            bias = jnp.where(seen, 0.0, neg_large)
            row = lax.broadcasted_iota(jnp.int32, (block, block), 0)
            col = lax.broadcasted_iota(jnp.int32, (block, block), 1)
            causal = jnp.where(col <= row, 0.0, neg_large)
            place = i * block + lax.broadcasted_iota(jnp.int32, (block, HEAD_SIZE), 0)
            prompt_values = with_ones(prompt_ref[1])
            cont_values = with_ones(cont_ref[1, 0, :extent])

            all_values = jnp.concatenate([prompt_values, cont_values], axis=0)

            def scores(h):
                q = q_ref[0, :, h * HEAD_SIZE : (h + 1) * HEAD_SIZE]
                first = lax.dot_general(
                    q, prompt_ref[0], contract_last, preferred_element_type=jnp.float32
                )
                second = lax.dot_general(
                    q, cont_ref[0, 0, :extent], contract_last, preferred_element_type=jnp.float32
                )
                first = first + bias
                diagonal = second[:, i * block :] + causal
                if i:
                    second = jnp.concatenate([second[:, : i * block], diagonal], axis=1)
                else:
                    second = diagonal
                return first, second

            def finish(h, first, second):
                row_max = jnp.maximum(
                    jnp.max(first, axis=1, keepdims=True), jnp.max(second, axis=1, keepdims=True)
                )
                first = jnp.exp2((first - row_max) * factor).astype(jnp.bfloat16)
                second = jnp.exp2((second - row_max) * factor).astype(jnp.bfloat16)
                total = jnp.dot(
                    jnp.concatenate([first, second], axis=1),
                    all_values,
                    preferred_element_type=jnp.float32,
                )
                mixed = total[:, :HEAD_SIZE] / total[:, HEAD_SIZE:]
                out_ref[0, :, h * HEAD_SIZE : (h + 1) * HEAD_SIZE] = jnp.where(
                    place < length, mixed, 0.0
                ).astype(out_ref.dtype)

            held = scores(0)
            for h in range(heads):
                following = scores(h + 1) if h + 1 < heads else None
                finish(h, *held)
                held = following


def attend(queries, own_prompt, own_cont, page_owner, lengths, offsets, base):
    here, cont_len, width = queries.shape
    prompt_len = own_prompt.shape[1]
    block = math.gcd(query_block, cont_len)
    return pl.pallas_call(
        functools.partial(attend_kernel, block),
        out_shape=jax.ShapeDtypeStruct(queries.shape, queries.dtype),
        grid_spec=pltpu.PrefetchScalarGridSpec(
            num_scalar_prefetch=3,
            grid=(here, cont_len // block),
            in_specs=[
                pl.BlockSpec((1, prompt_len), lambda s, i, *_: (0, 0)),
                pl.BlockSpec((1, block, width), lambda s, i, *_: (s, i, 0)),
                pl.BlockSpec((2, prompt_len, HEAD_SIZE), lambda s, i, *_: (0, 0, 0)),
                pl.BlockSpec((2, 1, cont_len, HEAD_SIZE), lambda s, i, *_: (0, s, 0, 0)),
            ],
            out_specs=pl.BlockSpec((1, block, width), lambda s, i, *_: (s, i, 0)),
        ),
        compiler_params=pltpu.CompilerParams(vmem_limit_bytes=60 * 1024 * 1024),
        name="attend",
    )(lengths, offsets, base, page_owner[None, :], queries, own_prompt, own_cont)


def solution(mesh):
    samples, ctx = mesh.shape["sample"], mesh.shape["ctx"]

    def local(queries, prompt, cont, page_owner, lengths, offsets):
        own_prompt, own_cont = gather(prompt, cont, samples, ctx)
        base = (lax.axis_index("sample") * queries.shape[0]).reshape(1)
        return attend(queries, own_prompt, own_cont, page_owner, lengths, offsets, base)

    in_specs = (
        P("sample", None, "ctx"),
        P(None, "ctx", "sample"),
        P(None, "sample", "ctx", None),
        P(),
        P(),
        P(),
    )
    out_specs = P("sample", None, "ctx")
    return jax.shard_map(local, mesh=mesh, in_specs=in_specs, out_specs=out_specs, check_vma=False)
```
